512 devices in a mesh: slab: 128 (over y, z, core), sub: 4 (over x).
Axes of the slice: x: 4, y: 4, z: 16, core: 2. Of those that a mesh axis runs over, the one named last changes fastest.
Arguments:
- coefficients: bfloat16 [7, 6, 6, 1024, 12, 128], P(None, None, None, 'slab', 'sub'), may hold values from -1 to 1
- earlier: float32 [30, 6, 1024, 12, 128], P(None, None, 'slab', 'sub'), may hold values from -6 to 6
- start: float32 [6, 1024, 12, 128], P(None, 'slab', 'sub'), may hold values from -8 to 8
- shifts: float32 [5], replicated, may hold values from -0.3 to 0.3
Outputs:
- new_basis: float32 [6, 6, 1024, 12, 128], P(None, None, 'slab', 'sub')
- projection: float32 [30, 6], replicated
- triangle: float32 [6, 6], replicated
The draws below stay inside these ranges and needn't reach their ends.
All inputs are finite; a program needn't handle non-finite values.
Results may differ from the reference program's by a relative error of at most 0.0015.
Values may be sent and summed in bfloat16 or wider, within the bound.
No kernel may reach another device: no remote copies, remote signals or barrier semaphores. Data moves between devices by JAX's collectives and lax.ppermute only.
A program may use at most 64 MiB of HBM per device.

```python
import jax
import jax.numpy as jnp
from jax import lax

COMP = 6
STENCIL = 7
DEPTH = 5
BLOCK = 6
EARLIER = 30
NZ = 1024
NX = 12
NY = 128


def earlier_basis(key):
    base_key = jax.random.fold_in(key, 7)
    dims = (EARLIER, COMP, NZ, NX, NY)
    values = jnp.clip(jax.random.normal(base_key, dims, jnp.float32), -6.0, 6.0)
    return values


def draw_earlier(key, part):
    return earlier_basis(key)


def draw_start(key, part):
    basis_values = earlier_basis(key)
    mixing = jnp.clip(jax.random.normal(jax.random.fold_in(key, 11), (EARLIER,), jnp.float32), -3.0, 3.0)
    jitter = jnp.clip(jax.random.normal(jax.random.fold_in(key, 13), (COMP, NZ, NX, NY), jnp.float32), -6.0, 6.0)
    combined = 0.3 * jnp.tensordot(mixing, basis_values, axes=1) + 0.5 * jitter
    return jnp.clip(combined, -8.0, 8.0)


def block_scale(stream_key, shape, pieces, least, largest):
    def one(axis_at, parts):
        draws = jax.random.uniform(jax.random.fold_in(jax.random.fold_in(stream_key, 6), axis_at), (parts,), jnp.float32, least / len(pieces), largest / len(pieces))
        return jnp.repeat(jnp.exp(draws), shape[axis_at] // parts).reshape((-1,) + (1,) * (len(shape) - axis_at - 1))

    loudness = one(*pieces[0])
    for cut in pieces[1:]:
        loudness = loudness * one(*cut)
    return loudness


def normal_values(stream_key, shape, scale, most, cuts=(), held_as=jnp.bfloat16):
    factor_of = block_scale(stream_key, shape, cuts, -0.22, 0.18) if cuts else 1.0
    values = jax.random.normal(stream_key, shape, jnp.float32) * scale * factor_of
    return jnp.minimum(jnp.maximum(values, -most), most).astype(held_as)


def setup_inputs(seed: int = 0) -> dict:
    key_of = jax.random.split(jax.random.key(seed), 5)
    return {
        "coefficients": normal_values(key_of[0], (STENCIL, COMP, COMP, NZ, NX, NY), (STENCIL * COMP) ** -0.5, 1.0, ((3, 128), (4, 4))),
        "earlier": draw_earlier(jax.random.fold_in(key_of[4], 71), 0),
        "start": draw_start(jax.random.fold_in(key_of[4], 71), 0),
        "shifts": jnp.clip(jax.random.uniform(key_of[3], (DEPTH,), jnp.float32, -0.3, 0.3), -0.3, 0.3),
    }


def nearby_fields(padded):
    center = padded[:, 1:-1, 1:-1]
    zeros_edge = jnp.zeros_like(center[..., :1])
    lower_y = jnp.concatenate([zeros_edge, center[..., :-1]], axis=3)
    upper_y = jnp.concatenate([center[..., 1:], zeros_edge], axis=3)
    return [center, padded[:, :-2, 1:-1], padded[:, 2:, 1:-1], padded[:, 1:-1, :-2], padded[:, 1:-1, 2:], lower_y, upper_y]

def apply_padded(coefficients, padded, theta):
    fields = nearby_fields(padded)
    result = (1.0 - theta) * fields[0]
    for coupling in range(len(fields)):
        result = result + jnp.sum(coefficients[coupling] * fields[coupling][None], axis=1)
    return result

def reference(coefficients, earlier, start, shifts):
    current = start
    vectors = [start]
    for step in range(DEPTH):
        padded = jnp.pad(current, ((0, 0), (1, 1), (1, 1), (0, 0)))
        current = apply_padded(coefficients, padded, shifts[step])
        vectors.append(current)
    basis = jnp.stack(vectors)
    flat = basis.reshape(BLOCK, -1)
    earlier_flat = earlier.reshape(EARLIER, -1)
    count = flat.shape[1]
    projection = jnp.dot(earlier_flat, flat.T, precision=lax.Precision.HIGHEST) / count
    rest = flat - jnp.dot(projection.T, earlier_flat, precision=lax.Precision.HIGHEST)
    gram = jnp.dot(rest, rest.T, precision=lax.Precision.HIGHEST) / count
    lower = jnp.linalg.cholesky(gram)
    new_flat = lax.linalg.triangular_solve(lower, rest, left_side=True, lower=True)
    return (new_flat.reshape(basis.shape), projection, lower.T)
```

```python
import jax
import jax.numpy as jnp
from jax import lax
from jax.experimental import pallas as pl
from jax.experimental.pallas import tpu as pltpu
from jax.sharding import Mesh
from jax.sharding import PartitionSpec as P

SLAB = ("slab_0", "slab_1", "slab_2")
NEAR = ("slab_0", "slab_2", "sub")
FAR = ("slab_1",)
EXACT = lax.Precision.HIGHEST


def chain(count):
    up = [(i, i + 1) for i in range(count - 1)]
    return up, [(b, a) for a, b in up]


def over_copies(x, axis):
    copies = jnp.broadcast_to(x, (lax.axis_size(axis), *x.shape))
    everything = lax.all_to_all(copies, axis, split_axis=0, concat_axis=0, tiled=True)
    return jnp.sum(everything, axis=0)


def packed_total(arrays):
    ravelled, at, done = (jnp.concatenate([a.reshape(-1) for a in arrays]), 0, [])
    so_far = over_copies(over_copies(ravelled[None], NEAR), FAR)[0]
    for a in arrays:
        done.append(so_far[at : at + a.size].reshape(a.shape))
        at += a.size
    return tuple(done)


def swap_halves(x):
    return pltpu.roll(x, x.shape[0] // 2, 0)


def half_mask(shape):
    return lax.broadcasted_iota(jnp.int32, shape, len(shape) - 2) < shape[-2] // 2


def pack(c_ref, s_ref, own_ref, lo_ref, hi_ref, start_ref, sems):
    parts = sems.shape[0]
    size = c_ref.shape[0] // parts
    copies = [
        pltpu.make_async_copy(
            c_ref.at[pl.ds(n * size, size)], own_ref.at[pl.ds(n * size, size)], sems.at[n]
        )
        for n in range(parts)
    ]
    for copy in copies:
        copy.start()
    start_ref[...] = s_ref[...]
    first = half_mask(c_ref.shape[2:])

    def pair(p, carry):
        a, b = own_ref[p, 0].astype(jnp.float32), own_ref[p, 1].astype(jnp.float32)
        hi_ref[p] = jnp.where(first, a, swap_halves(b)).astype(hi_ref.dtype)
        lo_ref[p] = jnp.where(first, swap_halves(a), b).astype(lo_ref.dtype)
        return carry

    for n, copy in enumerate(copies):
        copy.wait()
        lax.fori_loop(n * size, (n + 1) * size, pair, 0, unroll=9)


def unpack(lo_ref, hi_ref, wide_ref):
    first = half_mask(lo_ref.shape[1:])

    def pair(p, carry):
        lo, hi = lo_ref[p].astype(jnp.float32), hi_ref[p].astype(jnp.float32)
        wide_ref[p, 0] = jnp.where(first, hi, swap_halves(lo)).astype(wide_ref.dtype)
        wide_ref[p, 1] = jnp.where(first, swap_halves(hi), lo).astype(wide_ref.dtype)
        return carry

    lax.fori_loop(0, lo_ref.shape[0], pair, 0, unroll=9)


def in_vmem(x):
    return pltpu.with_memory_space_constraint(x, pltpu.VMEM)


def in_hbm(x):
    return pltpu.with_memory_space_constraint(x, pltpu.HBM)


VMEM = pl.BlockSpec(memory_space=pltpu.VMEM)
ANY = pl.BlockSpec(memory_space=pl.ANY)
SMEM = pl.BlockSpec(memory_space=pltpu.SMEM)
LIMIT = pltpu.CompilerParams(vmem_limit_bytes=2 * 2**20)


def cost(flops, size):
    return pl.CostEstimate(flops=flops, bytes_accessed=size, transcendentals=0)


def packed(coefficients, start):
    pairs = coefficients.reshape(-1, 2, *coefficients.shape[-2:])
    half = pltpu.VMEM((pairs.shape[0], *pairs.shape[2:]), pairs.dtype)
    return pl.pallas_call(
        pack,
        out_shape=(
            pltpu.VMEM(pairs.shape, pairs.dtype), half, half, pltpu.VMEM(start.shape, start.dtype)
        ),
        in_specs=[pl.BlockSpec(memory_space=pltpu.HBM), VMEM],
        out_specs=(VMEM,) * 4,
        scratch_shapes=[pltpu.SemaphoreType.DMA((6,))],
        compiler_params=LIMIT,
        cost_estimate=cost(10**6, 4 * 10**6),
    )(in_hbm(pairs), in_vmem(start))


def unpacked(lo, hi):
    return pl.pallas_call(
        unpack,
        out_shape=pltpu.VMEM((lo.shape[0], 2, *lo.shape[1:]), lo.dtype),
        in_specs=[VMEM] * 2,
        out_specs=VMEM,
        compiler_params=LIMIT,
        cost_estimate=cost(10**6, 4 * 10**6),
    )(in_vmem(lo), in_vmem(hi))


def is_odd():
    return lax.rem(lax.axis_index("sub"), 2) > 0


def begin_kernel(s_ref, lo_ref, hi_ref, v_ref, one_ref, two_ref):
    columns = s_ref.shape[1]
    v_ref[0] = s_ref[...]
    v_ref[1] = jnp.where(half_mask(s_ref.shape), hi_ref[...], lo_ref[...])
    odd = is_odd()
    near, far = v_ref[:, :, 0], v_ref[:, :, columns - 1]
    one_ref[...] = jnp.where(odd, near, far)
    two_ref[...] = jnp.where(odd, far, near)


def begun(start, s_lo, s_hi):
    edge = pltpu.VMEM((2, start.shape[0], *start.shape[2:]), start.dtype)
    return pl.pallas_call(
        begin_kernel,
        out_shape=(pltpu.VMEM((2, *start.shape), start.dtype), edge, edge),
        in_specs=[VMEM] * 3,
        out_specs=(VMEM,) * 3,
        compiler_params=LIMIT,
        cost_estimate=cost(10**5, 10**5),
    )(*(in_vmem(x) for x in (start, s_lo, s_hi)))


def early_kernel(e_ref, s_ref, held_ref, start_ref, sem):
    copy = pltpu.make_async_copy(e_ref, held_ref, sem.at[0])
    copy.start()
    start_ref[...] = s_ref[...]
    copy.wait()


def held(earlier, start):
    return pl.pallas_call(
        early_kernel,
        out_shape=(pltpu.VMEM(earlier.shape, earlier.dtype), pltpu.VMEM(start.shape, start.dtype)),
        in_specs=[pl.BlockSpec(memory_space=pltpu.HBM), VMEM],
        out_specs=(VMEM,) * 2,
        scratch_shapes=[pltpu.SemaphoreType.DMA((1,))],
        compiler_params=LIMIT,
        cost_estimate=cost(10**5, 5 * 10**6),
    )(in_hbm(earlier), in_vmem(start))


def step_kernel(step, first_step, last_step, shifts_ref, *refs):
    split = len(refs) - (1 if last_step else 3)
    (own_ref, wide_ref, v_ref, one_ref, two_ref, *more), outs = refs[:split], refs[split:]
    odd = is_odd()
    comps, columns = v_ref.shape[1:3]
    rows, lanes = v_ref.shape[3:]
    keep = 1.0 - shifts_ref[step]
    row = lax.broadcasted_iota(jnp.int32, (rows, lanes), 0)
    lane = lax.broadcasted_iota(jnp.int32, (rows, lanes), 1)
    for x in range(columns):
        acc = [[None] * comps for _ in range(1 if last_step else 2)]
        for e in range(comps):
            own, ext = v_ref[0, e, x], v_ref[1, e, x]
            down, up = pltpu.roll(own, 1, 0), pltpu.roll(own, rows - 1, 0)
            ext_down, ext_up = pltpu.roll(ext, 1, 0), pltpu.roll(ext, rows - 1, 0)
            if first_step:
                lo, hi = more[0][e, x], more[1][e, x]
                low = row < rows // 2
                wide_down = jnp.where(low, pltpu.roll(hi, 1, 0), pltpu.roll(lo, 1, 0))
                wide_up = jnp.where(low, pltpu.roll(hi, rows - 1, 0), pltpu.roll(lo, rows - 1, 0))
            else:
                wide_down, wide_up = ext_down, ext_up
            below = [jnp.where(row == 0, ext_down, down), jnp.where(row == 0, down, wide_down)]
            above = [
                jnp.where(row == rows - 1, ext_up, up),
                jnp.where(row == rows - 1, up, wide_up),
            ]
            for t, source in enumerate((own_ref, wide_ref)[: len(acc)]):
                center = v_ref[t, e, x]
                fields = [
                    center,
                    below[t],
                    above[t],
                    jnp.where(odd, one_ref[t, e], two_ref[t, e]) if x == 0 else v_ref[t, e, x - 1],
                    jnp.where(odd, two_ref[t, e], one_ref[t, e])
                    if x == columns - 1
                    else v_ref[t, e, x + 1],
                    jnp.where(lane == 0, 0.0, pltpu.roll(center, 1, 1)),
                    jnp.where(lane == lanes - 1, 0.0, pltpu.roll(center, lanes - 1, 1)),
                ]
                for c in range(comps):
                    total = acc[t][c]
                    for d, f in enumerate(fields):
                        term = source[d, c, e, x].astype(jnp.float32) * f
                        total = term if total is None else total + term
                    acc[t][c] = total
        for t in range(len(acc)):
            for c in range(comps):
                value = acc[t][c] + keep * v_ref[t, c, x]
                if last_step:
                    outs[0][c, x] = value
                else:
                    outs[0][t, c, x] = value
    if not last_step:
        for t in range(2):
            for c in range(comps):
                near, far = outs[0][t, c, 0], outs[0][t, c, columns - 1]
                outs[1][t, c] = jnp.where(odd, near, far)
                outs[2][t, c] = jnp.where(odd, far, near)


def stepped(step, depth, shifts, own, wide, v, one, two, more, after):
    last = step == depth - 1
    full = pltpu.VMEM(v.shape[1:] if last else v.shape, v.dtype)
    edge = pltpu.VMEM(one.shape, one.dtype)
    return pl.pallas_call(
        lambda *refs: step_kernel(
            step, step == 0, last, *refs[: 6 + len(more)], *refs[6 + len(more) + len(after) :]
        ),
        out_shape=(full,) if last else (full, edge, edge),
        in_specs=[SMEM] + [VMEM] * (5 + len(more)) + [ANY] * len(after),
        out_specs=(VMEM,) if last else (VMEM,) * 3,
        compiler_params=LIMIT,
        cost_estimate=cost(10**7, 3 * 10**6),
    )(shifts, *(in_vmem(a) for a in (own, wide, v, one, two, *more)), *after)


def dots_kernel(e_ref, *refs):
    *w_refs, out_ref, part = refs
    count, comps, columns = e_ref.shape[:3]
    v_ref = w_refs[-1]
    part[...] = jnp.zeros_like(part)
    group = 6
    terms = [(e_ref, j) for j in range(count)] + [(w, None) for w in w_refs]
    for at in range(0, len(terms), group):
        some = terms[at : at + group]
        acc = [None] * len(some)
        for c in range(comps):
            for x in range(columns):
                v = v_ref[c, x]
                for n, (ref, j) in enumerate(some):
                    term = v * (ref[c, x] if j is None else ref[j, c, x])
                    acc[n] = term if acc[n] is None else acc[n] + term
        for n, total in enumerate(acc):
            part[at + n : at + n + 1] = jnp.sum(total, axis=0, keepdims=True)
    ones = jnp.ones((8, part.shape[1]), jnp.float32)
    out_ref[...] = lax.dot_general(
        ones, part[...], (((1,), (1,)), ((), ())), precision=EXACT,
        preferred_element_type=jnp.float32,
    )[:1]


def dots(earlier, vectors):
    width = 40
    return pl.pallas_call(
        dots_kernel,
        out_shape=pltpu.VMEM((1, width), jnp.float32),
        in_specs=[VMEM] * (1 + len(vectors)),
        out_specs=VMEM,
        scratch_shapes=[pltpu.VMEM((width, vectors[0].shape[-1]), jnp.float32)],
        compiler_params=LIMIT,
        cost_estimate=cost(10**6, 3 * 10**6),
    )(in_vmem(earlier), *(in_vmem(v) for v in vectors))


def finish(cross_ref, turned_ref, self_ref, early_ref, e_ref, *refs):
    block = self_ref.shape[0]
    w_refs, (out_ref, proj_ref, tri_ref, o_vmem, small, spread, sems) = refs[:block], refs[block:]
    count = cross_ref.shape[0]
    p = cross_ref[...]
    proj = pltpu.make_async_copy(turned_ref, proj_ref, sems.at[0])
    proj.start()
    part = jnp.dot(early_ref[...], p, precision=EXACT) - 2.0 * p
    gram = self_ref[...] + jnp.dot(turned_ref[...], part, precision=EXACT)
    row = lax.broadcasted_iota(jnp.int32, (block, block), 0)
    col = lax.broadcasted_iota(jnp.int32, (block, block), 1)
    unit = jnp.where(row == col, 1.0, 0.0)
    a = jnp.concatenate([gram, unit, -turned_ref[...]], axis=1)
    rows = lax.broadcasted_iota(jnp.int32, a.shape, 0)
    for k in range(block):
        scale = 1.0 / jnp.sqrt(a[k : k + 1, k : k + 1])
        pivot = a[k : k + 1] * scale
        factor = a[:, k : k + 1] * scale
        a = jnp.where(rows == k, pivot, jnp.where(rows > k, a - factor * pivot, a))
    small[...] = jnp.where(row <= col, a[:, :block], 0.0)
    tri = pltpu.make_async_copy(small, tri_ref, sems.at[1])
    tri.start()
    shape = spread.shape[2:]
    for k in range(block):
        for i in range(block + count):
            if i >= block or i <= k:
                at = block + i
                spread[i, k] = jnp.broadcast_to(a[k : k + 1, at : at + 1], shape)
    outs = []
    comps = 2
    for g in range(e_ref.shape[1] // comps):
        sel = slice(g * comps, (g + 1) * comps)
        acc = [None] * block
        for i in range(block + count):
            x = w_refs[i][sel] if i < block else e_ref[i - block, sel]
            for k in range(block):
                if i >= block or i <= k:
                    t = spread[i, k][None, None] * x
                    acc[k] = t if acc[k] is None else acc[k] + t
        for k in range(block):
            o_vmem[g, k] = acc[k]
        c = pltpu.make_async_copy(o_vmem.at[g], out_ref.at[:, sel], sems.at[2 + g])
        c.start()
        outs.append(c)
    for c in [proj, tri, *outs]:
        c.wait()


def finished(cross, turned, self_sum, early, vectors, earlier):
    block = len(vectors)
    fields, *rest = vectors[0].shape
    return pl.pallas_call(
        finish,
        out_shape=(
            pltpu.HBM((block, fields, *rest), jnp.float32),
            pltpu.HBM(turned.shape, jnp.float32),
            pltpu.HBM(self_sum.shape, jnp.float32),
        ),
        in_specs=[VMEM] * (5 + block),
        out_specs=(pl.BlockSpec(memory_space=pltpu.HBM),) * 3,
        scratch_shapes=[
            pltpu.VMEM((fields // 2, block, 2, *rest), jnp.float32),
            pltpu.VMEM(self_sum.shape, jnp.float32),
            pltpu.VMEM((block + earlier.shape[0], block, *rest[1:]), jnp.float32),
            pltpu.SemaphoreType.DMA((2 + fields // 2,)),
        ],
        compiler_params=LIMIT,
        cost_estimate=cost(10**7, 3 * 10**6),
    )(*(in_vmem(x) for x in (cross, turned, self_sum, early, earlier, *vectors)))


def body(coefficients, earlier, start, shifts):
    depth = shifts.shape[0]
    coefficients = jnp.transpose(coefficients, (0, 1, 2, 4, 3, 5))
    earlier = jnp.transpose(earlier, (0, 1, 3, 2, 4))
    start = jnp.transpose(start, (0, 2, 1, 3))
    up, down = chain(lax.axis_size(SLAB))
    columns = lax.axis_size("sub")
    pairs = [(i, i ^ 1) for i in range(columns)]
    between = [(i, ((i + 1) ^ 1) - 1) for i in range(1, columns - 1)]
    own, lo, hi, start = packed(coefficients, start)
    lo = lax.ppermute(lo, SLAB, up)
    hi = lax.ppermute(hi, SLAB, down)
    earlier, start = held(earlier, start)
    s_lo = lax.ppermute(start, SLAB, up)
    s_hi = lax.ppermute(start, SLAB, down)
    own = own.reshape(coefficients.shape)
    wide = unpacked(lo, hi).reshape(coefficients.shape)
    v, one, two = begun(start, s_lo, s_hi)
    vectors, rows, early = [start], [], []
    thirds = earlier.shape[1] // 3
    for step in range(depth):
        from_one = lax.ppermute(one, "sub", pairs)
        from_two = lax.ppermute(two, "sub", between)
        rows.append(dots(earlier, vectors))
        more = (s_lo, s_hi) if step == 0 else ()
        after = [rows[-1]]
        if 1 <= step <= 3:
            tied, v = lax.optimization_barrier((earlier, v))
            some = tied[:, (step - 1) * thirds : step * thirds].reshape(tied.shape[0], -1)
            early.append(lax.optimization_barrier(jnp.dot(some, some.T, precision=EXACT)))
            after.append(early[-1])
        out = stepped(step, depth, shifts, own, wide, v, from_one, from_two, more, after)
        if step < depth - 1:
            v, one, two = out
            vectors.append(v[0])
        else:
            vectors.append(out[0])
    rows.append(dots(earlier, vectors))
    block = len(vectors)
    count = start.size * lax.axis_size(SLAB) * lax.axis_size("sub")
    rows, early = lax.optimization_barrier((rows, early))
    rows = jnp.concatenate(rows, axis=0)
    n = earlier.shape[0]
    cross, square, early = packed_total((rows[:, :n], rows[:, n : n + block], sum(early)))
    turned = cross / count
    i = jnp.arange(block)
    own_sum = jnp.where(i[:, None] >= i[None], square, square.T) / count
    new, projection, triangle = finished(
        turned.T, turned, own_sum, early / count, vectors, earlier
    )
    return (jnp.transpose(new, (0, 1, 3, 2, 4)), projection.T, triangle)


def solution(mesh):
    torus = Mesh(
        mesh.devices.reshape(4, 16, 2, mesh.shape["sub"]), ("slab_0", "slab_1", "slab_2", "sub")
    )
    return jax.shard_map(
        body,
        mesh=torus,
        in_specs=(
            P(None, None, None, SLAB, "sub", None),
            P(None, None, SLAB, "sub", None),
            P(None, SLAB, "sub", None),
            P(),
        ),
        out_specs=(P(None, None, SLAB, "sub", None), P(), P()),
        check_vma=False,
    )
```

```python
import jax
import jax.numpy as jnp
from jax import lax
from jax.experimental import pallas as pl
from jax.experimental.pallas import tpu as pltpu
from jax.sharding import Mesh
from jax.sharding import PartitionSpec as P

SLAB = ("slab_0", "slab_1", "slab_2")
NEAR = ("slab_0", "slab_2", "sub")
FAR = ("slab_1",)
EXACT = lax.Precision.HIGHEST


def chain(count):
    up = [(i, i + 1) for i in range(count - 1)]
    return up, [(b, a) for a, b in up]


def all_copies(x, axis):
    copies = jnp.broadcast_to(x, (lax.axis_size(axis), *x.shape))
    return lax.all_to_all(copies, axis, split_axis=0, concat_axis=0, tiled=True)


def over_copies(x, axis):
    return jnp.sum(all_copies(x, axis), axis=0)


def swap_halves(x):
    return pltpu.roll(x, x.shape[0] // 2, 0)


def half_mask(shape):
    return lax.broadcasted_iota(jnp.int32, shape, len(shape) - 2) < shape[-2] // 2


def pack(c_ref, s_ref, own_ref, lo_ref, hi_ref, start_ref, one_ref, two_ref, raw, sems):
    parts = sems.shape[0] - 1
    begin = pltpu.make_async_copy(s_ref, start_ref, sems.at[parts])
    begin.start()
    size = c_ref.shape[0] // parts
    copies = [
        pltpu.make_async_copy(
            c_ref.at[pl.ds(n * size, size)], raw.at[pl.ds(n * size, size)], sems.at[n]
        )
        for n in range(parts)
    ]
    for copy in copies:
        copy.start()
    first = half_mask(c_ref.shape[2:])

    def pair(p, carry):
        a, b = raw[p, 0].astype(jnp.float32), raw[p, 1].astype(jnp.float32)
        own_ref[p, 0] = a
        own_ref[p, 1] = b
        hi_ref[p] = jnp.where(first, a, swap_halves(b)).astype(hi_ref.dtype)
        lo_ref[p] = jnp.where(first, swap_halves(a), b).astype(lo_ref.dtype)
        return carry

    for n, copy in enumerate(copies):
        copy.wait()
        lax.fori_loop(n * size, (n + 1) * size, pair, 0, unroll=9)
    begin.wait()
    odd = is_odd()
    near, far = start_ref[:, 0], start_ref[:, start_ref.shape[1] - 1]
    one_ref[...] = jnp.where(odd, near, far)
    two_ref[...] = jnp.where(odd, far, near)


def unpack(lo_ref, hi_ref, wide_ref):
    first = half_mask(lo_ref.shape[1:])

    def pair(p, carry):
        lo, hi = lo_ref[p].astype(jnp.float32), hi_ref[p].astype(jnp.float32)
        wide_ref[p, 0] = jnp.where(first, hi, swap_halves(lo))
        wide_ref[p, 1] = jnp.where(first, swap_halves(hi), lo)
        return carry

    lax.fori_loop(0, lo_ref.shape[0], pair, 0, unroll=9)


def in_vmem(x):
    return pltpu.with_memory_space_constraint(x, pltpu.VMEM)


def in_hbm(x):
    return pltpu.with_memory_space_constraint(x, pltpu.HBM)


VMEM = pl.BlockSpec(memory_space=pltpu.VMEM)
ANY = pl.BlockSpec(memory_space=pl.ANY)
SMEM = pl.BlockSpec(memory_space=pltpu.SMEM)
LIMIT = pltpu.CompilerParams(vmem_limit_bytes=2 * 2**20)


def cost(flops, size):
    return pl.CostEstimate(flops=flops, bytes_accessed=size, transcendentals=0)


def packed(coefficients, start):
    pairs = coefficients.reshape(-1, 2, *coefficients.shape[-2:])
    half = pltpu.VMEM((pairs.shape[0], *pairs.shape[2:]), pairs.dtype)
    edge = pltpu.VMEM((start.shape[0], *start.shape[2:]), start.dtype)
    return pl.pallas_call(
        pack,
        out_shape=(
            pltpu.VMEM(pairs.shape, jnp.float32),
            half,
            half,
            pltpu.VMEM(start.shape, start.dtype),
            edge,
            edge,
        ),
        in_specs=[pl.BlockSpec(memory_space=pltpu.HBM)] * 2,
        out_specs=(VMEM,) * 6,
        scratch_shapes=[pltpu.VMEM(pairs.shape, pairs.dtype), pltpu.SemaphoreType.DMA((7,))],
        compiler_params=LIMIT,
        cost_estimate=cost(10**6, 4 * 10**6),
    )(in_hbm(pairs), in_hbm(start))


def unpacked(lo, hi):
    return pl.pallas_call(
        unpack,
        out_shape=pltpu.VMEM((lo.shape[0], 2, *lo.shape[1:]), jnp.float32),
        in_specs=[VMEM] * 2,
        out_specs=VMEM,
        compiler_params=LIMIT,
        cost_estimate=cost(10**6, 4 * 10**6),
    )(in_vmem(lo), in_vmem(hi))


def is_odd():
    return lax.rem(lax.axis_index("sub"), 2) > 0


def both_kernel(s_ref, one_ref, two_ref, up_ref, down_ref):
    odd = is_odd()
    columns = s_ref.shape[1]
    low = half_mask(s_ref.shape[2:])
    for e in range(s_ref.shape[0]):
        one, two = one_ref[e], two_ref[e]
        left, right = jnp.where(odd, one, two), jnp.where(odd, two, one)
        up_ref[e, :columns] = s_ref[e]
        down_ref[e, :columns] = s_ref[e]
        up_ref[e, columns] = jnp.where(low, swap_halves(left), right)
        down_ref[e, columns] = jnp.where(low, left, swap_halves(right))


def begin_kernel(s_ref, lo_ref, hi_ref, one_ref, two_ref, v_ref, first_ref, second_ref):
    odd = is_odd()
    columns = s_ref.shape[1]
    low = half_mask(s_ref.shape[2:])
    for e in range(s_ref.shape[0]):
        for x in range(columns):
            v_ref[0, e, x] = s_ref[e, x]
            v_ref[1, e, x] = jnp.where(low, hi_ref[e, x], lo_ref[e, x])
        lo, hi = lo_ref[e, columns], hi_ref[e, columns]
        left = jnp.where(low, hi, swap_halves(lo))
        right = jnp.where(low, swap_halves(hi), lo)
        first_ref[0, e], second_ref[0, e] = one_ref[e], two_ref[e]
        first_ref[1, e] = jnp.where(odd, left, right)
        second_ref[1, e] = jnp.where(odd, right, left)


def small_call(kernel, outs, *operands):
    return pl.pallas_call(
        kernel,
        out_shape=tuple(pltpu.VMEM(shape, jnp.float32) for shape in outs),
        in_specs=[VMEM] * len(operands),
        out_specs=(VMEM,) * len(outs),
        compiler_params=LIMIT,
        cost_estimate=cost(10**5, 10**5),
    )(*(in_vmem(x) for x in operands))


def early_kernel(e_ref, after_ref, held_ref, sem):
    copy = pltpu.make_async_copy(e_ref, held_ref, sem.at[0])
    copy.start()
    copy.wait()


def held(earlier, after):
    return pl.pallas_call(
        early_kernel,
        out_shape=pltpu.VMEM(earlier.shape, earlier.dtype),
        in_specs=[pl.BlockSpec(memory_space=pltpu.HBM), ANY],
        out_specs=VMEM,
        scratch_shapes=[pltpu.SemaphoreType.DMA((1,))],
        compiler_params=LIMIT,
        cost_estimate=cost(10**5, 5 * 10**6),
    )(in_hbm(earlier), after)


def step_kernel(step, first_step, last_step, shifts_ref, *refs):
    split = len(refs) - (1 if last_step else 3)
    (own_ref, wide_ref, v_ref, one_ref, two_ref, *more), outs = refs[:split], refs[split:]
    odd = is_odd()
    comps, columns = v_ref.shape[1:3]
    rows, lanes = v_ref.shape[3:]
    keep = 1.0 - shifts_ref[step]
    row = lax.broadcasted_iota(jnp.int32, (rows, lanes), 0)
    lane = lax.broadcasted_iota(jnp.int32, (rows, lanes), 1)
    for x in range(columns):
        acc = [[None] * comps for _ in range(1 if last_step else 2)]
        for e in range(comps):
            own, ext = v_ref[0, e, x], v_ref[1, e, x]
            down, up = pltpu.roll(own, 1, 0), pltpu.roll(own, rows - 1, 0)
            ext_down, ext_up = pltpu.roll(ext, 1, 0), pltpu.roll(ext, rows - 1, 0)
            if first_step:
                lo, hi = more[0][e, x], more[1][e, x]
                low = row < rows // 2
                wide_down = jnp.where(low, pltpu.roll(hi, 1, 0), pltpu.roll(lo, 1, 0))
                wide_up = jnp.where(low, pltpu.roll(hi, rows - 1, 0), pltpu.roll(lo, rows - 1, 0))
            else:
                wide_down, wide_up = ext_down, ext_up
            below = [jnp.where(row == 0, ext_down, down), jnp.where(row == 0, down, wide_down)]
            above = [
                jnp.where(row == rows - 1, ext_up, up),
                jnp.where(row == rows - 1, up, wide_up),
            ]
            for t, source in enumerate((own_ref, wide_ref)[: len(acc)]):
                center = v_ref[t, e, x]
                fields = [
                    center,
                    below[t],
                    above[t],
                    jnp.where(odd, one_ref[t, e], two_ref[t, e]) if x == 0 else v_ref[t, e, x - 1],
                    jnp.where(odd, two_ref[t, e], one_ref[t, e])
                    if x == columns - 1
                    else v_ref[t, e, x + 1],
                    jnp.where(lane == 0, 0.0, pltpu.roll(center, 1, 1)),
                    jnp.where(lane == lanes - 1, 0.0, pltpu.roll(center, lanes - 1, 1)),
                ]
                for c in range(comps):
                    total = acc[t][c]
                    for d, f in enumerate(fields):
                        term = source[d, c, e, x] * f
                        total = term if total is None else total + term
                    acc[t][c] = total
        for t in range(len(acc)):
            for c in range(comps):
                value = acc[t][c] + keep * v_ref[t, c, x]
                if last_step:
                    outs[0][c, x] = value
                else:
                    outs[0][t, c, x] = value
    if not last_step:
        for t in range(2):
            for c in range(comps):
                near, far = outs[0][t, c, 0], outs[0][t, c, columns - 1]
                outs[1][t, c] = jnp.where(odd, near, far)
                outs[2][t, c] = jnp.where(odd, far, near)


def stepped(step, depth, shifts, own, wide, v, one, two, more, after):
    last = step == depth - 1
    full = pltpu.VMEM(v.shape[1:] if last else v.shape, v.dtype)
    edge = pltpu.VMEM(one.shape, one.dtype)
    return pl.pallas_call(
        lambda *refs: step_kernel(
            step, step == 0, last, *refs[: 6 + len(more)], *refs[6 + len(more) + len(after) :]
        ),
        out_shape=(full,) if last else (full, edge, edge),
        in_specs=[SMEM] + [VMEM] * (5 + len(more)) + [ANY] * len(after),
        out_specs=(VMEM,) if last else (VMEM,) * 3,
        compiler_params=LIMIT,
        cost_estimate=cost(10**7, 3 * 10**6),
    )(shifts, *(in_vmem(a) for a in (own, wide, v, one, two, *more)), *after)


LANES = 128
SLOT = 32
STRIDE = 40


def dots_row(e_ref, w_refs, part):
    count, comps, columns = e_ref.shape[:3]
    v_ref = w_refs[-1]
    part[...] = jnp.zeros_like(part)
    group = 6
    terms = [(e_ref, j) for j in range(count)] + [(w, None) for w in w_refs]
    for at in range(0, len(terms), group):
        some = terms[at : at + group]
        acc = [None] * len(some)
        for c in range(comps):
            for x in range(columns):
                v = v_ref[c, x]
                for n, (ref, j) in enumerate(some):
                    term = v * (ref[c, x] if j is None else ref[j, c, x])
                    acc[n] = term if acc[n] is None else acc[n] + term
        for n, total in enumerate(acc):
            part[at + n : at + n + 1] = jnp.sum(total, axis=0, keepdims=True)
    ones = jnp.ones((8, part.shape[1]), jnp.float32)
    return lax.dot_general(
        ones, part[...], (((1,), (1,)), ((), ())), precision=EXACT,
        preferred_element_type=jnp.float32,
    )[:1]


def dots_kernel(e_ref, *refs):
    *w_refs, out_ref, part = refs
    out_ref[...] = dots_row(e_ref, w_refs, part)


def dots(earlier, vectors):
    return pl.pallas_call(
        dots_kernel,
        out_shape=pltpu.VMEM((1, LANES), jnp.float32),
        in_specs=[VMEM] * (1 + len(vectors)),
        out_specs=VMEM,
        scratch_shapes=[pltpu.VMEM((LANES, LANES), jnp.float32)],
        compiler_params=LIMIT,
        cost_estimate=cost(10**6, 3 * 10**6),
    )(in_vmem(earlier), *(in_vmem(v) for v in vectors))


def lane_roll(x, shift):
    shift %= LANES
    return pltpu.roll(x, shift, 1) if shift else x


def folds(count):
    for j in range(count // 2):
        yield j, count - 1 - j, j // (LANES // SLOT), SLOT * (j % (LANES // SLOT))


def tiles_of(count, block):
    early = -(-(count // 2) * SLOT // LANES)
    per = LANES // STRIDE
    return early, per, early + -(-block // per)


def message_kernel(block, sums, e_ref, *refs):
    w_refs, refs = refs[:block], refs[block:]
    rows, refs = refs[: block - 1], refs[block - 1 :]
    parts, (out_ref, part, square) = refs[:sums], refs[sums:]
    count = e_ref.shape[0]
    early, per, total = tiles_of(count, block)
    square[...] = jnp.zeros_like(square)
    square[:count, :count] = sum(p[...] for p in parts)
    lane = lax.broadcasted_iota(jnp.int32, (1, LANES), 1)
    tiles = [jnp.zeros((1, LANES), jnp.float32) for _ in range(total)]
    for j, r, q, at in folds(count):
        upper = lane_roll(square[j : j + 1], at + 1)
        lower = lane_roll(square[r : r + 1], at - r)
        tiles[q] = jnp.where(
            (lane > at + j) & (lane <= at + count),
            upper,
            jnp.where((lane >= at) & (lane <= at + j), lower, tiles[q]),
        )
    last = dots_row(e_ref, w_refs, part)
    for k in range(block):
        row = last if k == block - 1 else rows[k][...]
        t = early + k // per
        tiles[t] = tiles[t] + lane_roll(row, STRIDE * (k % per))
    for t in range(total):
        out_ref[:, t * LANES : (t + 1) * LANES] = tiles[t]


def message(earlier, vectors, rows, parts):
    count, block = earlier.shape[0], len(vectors)
    width = LANES * tiles_of(count, block)[2]
    operands = (earlier, *vectors, *rows, *parts)
    return pl.pallas_call(
        lambda *refs: message_kernel(block, len(parts), *refs),
        out_shape=pltpu.VMEM((1, width), jnp.float32),
        in_specs=[VMEM] * len(operands),
        out_specs=VMEM,
        scratch_shapes=[
            pltpu.VMEM((LANES, LANES), jnp.float32),
            pltpu.VMEM((SLOT, LANES), jnp.float32),
        ],
        compiler_params=LIMIT,
        cost_estimate=cost(10**6, 3 * 10**6),
    )(*(in_vmem(x) for x in operands))


def against(a, b):
    return lax.dot_general(
        a, b, (((1,), (1,)), ((), ())), precision=EXACT, preferred_element_type=jnp.float32
    )


def finish(block, scale, m_ref, e_ref, *refs):
    w_refs, refs = refs[:block], refs[block:]
    out_ref, proj_ref, tri_ref, o_vmem, small, turned_vmem, square, lines, spread, sems = refs
    count = e_ref.shape[0]
    early, per, total = tiles_of(count, block)
    tiles = [
        jnp.sum(m_ref[:, t * LANES : (t + 1) * LANES], axis=0, keepdims=True) * scale
        for t in range(total)
    ]
    lane = lax.broadcasted_iota(jnp.int32, (1, LANES), 1)
    for k in range(block):
        lines[k : k + 1] = lane_roll(tiles[early + k // per], -STRIDE * (k % per))
    for j, r, q, at in folds(count):
        upper = jnp.where(lane >= j, lane_roll(tiles[q], -at - 1), 0.0)
        lower = jnp.where(lane >= r, lane_roll(tiles[q], r - at), 0.0)
        square[j : j + 1] = jnp.where(lane == j, 0.5 * upper, upper)
        square[r : r + 1] = jnp.where(lane == r, 0.5 * lower, lower)
    turned = lines[:block, :count]
    turned_vmem[...] = turned
    proj = pltpu.make_async_copy(turned_vmem, proj_ref, sems.at[0])
    proj.start()
    row = lax.broadcasted_iota(jnp.int32, (block, block), 0)
    col = lax.broadcasted_iota(jnp.int32, (block, block), 1)
    unit = jnp.where(row == col, 1.0, 0.0)
    inner = lines[:block, count : count + block]
    inner = jnp.where(row > col, inner, jnp.where(row == col, 0.5 * inner, 0.0))
    part = jnp.dot(turned, square[:count, :count], precision=EXACT) - turned
    gram = inner + against(part, turned)
    gram = gram + against(unit, gram)
    a = jnp.concatenate([gram, unit, -turned], axis=1)
    rows = lax.broadcasted_iota(jnp.int32, a.shape, 0)
    for k in range(block):
        inverse = 1.0 / jnp.sqrt(a[k : k + 1, k : k + 1])
        pivot = a[k : k + 1] * inverse
        factor = a[:, k : k + 1] * inverse
        a = jnp.where(rows == k, pivot, jnp.where(rows > k, a - factor * pivot, a))
    small[...] = jnp.where(row <= col, a[:, :block], 0.0)
    tri = pltpu.make_async_copy(small, tri_ref, sems.at[1])
    tri.start()
    shape = spread.shape[2:]
    for k in range(block):
        for i in range(block + count):
            if i >= block or i <= k:
                at = block + i
                spread[i, k] = jnp.broadcast_to(a[k : k + 1, at : at + 1], shape)
    outs = []
    comps = 2
    for g in range(e_ref.shape[1] // comps):
        sel = slice(g * comps, (g + 1) * comps)
        acc = [None] * block
        for i in range(block + count):
            x = w_refs[i][sel] if i < block else e_ref[i - block, sel]
            for k in range(block):
                if i >= block or i <= k:
                    t = spread[i, k][None, None] * x
                    acc[k] = t if acc[k] is None else acc[k] + t
        for k in range(block):
            o_vmem[g, k] = acc[k]
        c = pltpu.make_async_copy(o_vmem.at[g], out_ref.at[:, sel], sems.at[2 + g])
        c.start()
        outs.append(c)
    for c in [proj, tri, *outs]:
        c.wait()


def finished(everything, total, vectors, earlier):
    block, count = len(vectors), earlier.shape[0]
    fields, *rest = vectors[0].shape
    operands = (everything, earlier, *vectors)
    return pl.pallas_call(
        lambda *refs: finish(block, 1.0 / total, *refs),
        out_shape=(
            pltpu.HBM((block, fields, *rest), jnp.float32),
            pltpu.HBM((block, count), jnp.float32),
            pltpu.HBM((block, block), jnp.float32),
        ),
        in_specs=[VMEM] * len(operands),
        out_specs=(pl.BlockSpec(memory_space=pltpu.HBM),) * 3,
        scratch_shapes=[
            pltpu.VMEM((fields // 2, block, 2, *rest), jnp.float32),
            pltpu.VMEM((block, block), jnp.float32),
            pltpu.VMEM((block, count), jnp.float32),
            pltpu.VMEM((SLOT, LANES), jnp.float32),
            pltpu.VMEM((8, LANES), jnp.float32),
            pltpu.VMEM((block + count, block, *rest[1:]), jnp.float32),
            pltpu.SemaphoreType.DMA((2 + fields // 2,)),
        ],
        compiler_params=LIMIT,
        cost_estimate=cost(10**7, 3 * 10**6),
    )(*(in_vmem(x) for x in operands))


def body(coefficients, earlier, start, shifts):
    depth = shifts.shape[0]
    coefficients = jnp.transpose(coefficients, (0, 1, 2, 4, 3, 5))
    earlier = jnp.transpose(earlier, (0, 1, 3, 2, 4))
    start = jnp.transpose(start, (0, 2, 1, 3))
    up, down = chain(lax.axis_size(SLAB))
    columns = lax.axis_size("sub")
    pairs = [(i, i ^ 1) for i in range(columns)]
    between = [(i, ((i + 1) ^ 1) - 1) for i in range(1, columns - 1)]
    own, lo, hi, start, one, two = packed(coefficients, start)
    lo = lax.ppermute(lo, SLAB, up)
    hi = lax.ppermute(hi, SLAB, down)
    fields, width, *plane = start.shape
    from_one = lax.ppermute(one, "sub", pairs)
    from_two = lax.ppermute(two, "sub", between)
    s_lo, s_hi = small_call(
        both_kernel, [(fields, width + 1, *plane)] * 2, start, from_one, from_two
    )
    earlier = held(earlier, s_hi)
    s_lo = lax.ppermute(s_lo, SLAB, up)
    s_hi = lax.ppermute(s_hi, SLAB, down)
    own = own.reshape(coefficients.shape)
    wide = unpacked(lo, hi).reshape(coefficients.shape)
    v, from_one, from_two = small_call(
        begin_kernel,
        [(2, *start.shape)] + [(2, fields, *plane)] * 2,
        start, s_lo, s_hi, from_one, from_two,
    )
    vectors, rows, early = [start], [], []
    thirds = earlier.shape[1] // 3
    for step in range(depth):
        if step:
            from_one = lax.ppermute(one, "sub", pairs)
            from_two = lax.ppermute(two, "sub", between)
        rows.append(dots(earlier, vectors))
        more = (s_lo, s_hi) if step == 0 else ()
        after = [rows[-1]]
        if 1 <= step <= 3:
            tied, v = lax.optimization_barrier((earlier, v))
            some = tied[:, (step - 1) * thirds : step * thirds].reshape(tied.shape[0], -1)
            early.append(lax.optimization_barrier(jnp.dot(some, some.T, precision=EXACT)))
            after.append(early[-1])
        out = stepped(step, depth, shifts, own, wide, v, from_one, from_two, more, after)
        if step < depth - 1:
            v, one, two = out
            vectors.append(v[0])
        else:
            vectors.append(out[0])
    total = start.size * lax.axis_size(SLAB) * lax.axis_size("sub")
    near = over_copies(message(earlier, vectors, rows, early), NEAR)
    everything = all_copies(near, FAR)[:, 0]
    new, projection, triangle = finished(everything, total, vectors, earlier)
    return (jnp.transpose(new, (0, 1, 3, 2, 4)), projection.T, triangle)


def solution(mesh):
    torus = Mesh(
        mesh.devices.reshape(4, 16, 2, mesh.shape["sub"]), ("slab_0", "slab_1", "slab_2", "sub")
    )
    return jax.shard_map(
        body,
        mesh=torus,
        in_specs=(
            P(None, None, None, SLAB, "sub", None),
            P(None, None, SLAB, "sub", None),
            P(None, SLAB, "sub", None),
            P(),
        ),
        out_specs=(P(None, None, SLAB, "sub", None), P(), P()),
        check_vma=False,
    )
```

```python
import jax
import jax.numpy as jnp
from jax import lax
from jax.experimental import pallas as pl
from jax.experimental.pallas import tpu as pltpu
from jax.sharding import Mesh
from jax.sharding import PartitionSpec as P

SLAB = ("slab_0", "slab_1", "slab_2")
NEAR = ("slab_0", "slab_2", "sub")
FAR = ("slab_1",)
EXACT = lax.Precision.HIGHEST


def all_copies(x, axis):
    copies = jnp.broadcast_to(x, (lax.axis_size(axis), *x.shape))
    return lax.all_to_all(copies, axis, split_axis=0, concat_axis=0, tiled=True)


def over_copies(x, axis):
    return jnp.sum(all_copies(x, axis), axis=0)


def swap_halves(x):
    return pltpu.roll(x, x.shape[0] // 2, 0)


def half_mask(shape):
    return lax.broadcasted_iota(jnp.int32, shape, len(shape) - 2) < shape[-2] // 2


def is_odd():
    return lax.rem(lax.axis_index("sub"), 2) > 0


def is_upper():
    return lax.axis_index("slab_2") > 0


def pack(c_ref, s_ref, own_ref, inner_ref, outer_ref, start_ref, one_ref, two_ref, raw, sems):
    parts = sems.shape[0] - 1
    begin = pltpu.make_async_copy(s_ref, start_ref, sems.at[parts])
    begin.start()
    size = c_ref.shape[0] // parts
    copies = [
        pltpu.make_async_copy(
            c_ref.at[pl.ds(n * size, size)], raw.at[pl.ds(n * size, size)], sems.at[n]
        )
        for n in range(parts)
    ]
    for copy in copies:
        copy.start()
    first = half_mask(c_ref.shape[2:])
    upper = is_upper()

    def pair(p, carry):
        a, b = raw[p, 0].astype(jnp.float32), raw[p, 1].astype(jnp.float32)
        own_ref[p, 0] = a
        own_ref[p, 1] = b
        down = jnp.where(first, a, swap_halves(b))
        up = jnp.where(first, swap_halves(a), b)
        inner_ref[p] = jnp.where(upper, down, up).astype(inner_ref.dtype)
        outer_ref[p] = jnp.where(upper, up, down).astype(outer_ref.dtype)
        return carry

    for n, copy in enumerate(copies):
        copy.wait()
        lax.fori_loop(n * size, (n + 1) * size, pair, 0, unroll=9)
    begin.wait()
    odd = is_odd()
    near, far = start_ref[:, 0], start_ref[:, start_ref.shape[1] - 1]
    one_ref[...] = jnp.where(odd, near, far)
    two_ref[...] = jnp.where(odd, far, near)


def unpack(inner_ref, outer_ref, wide_ref):
    first = half_mask(inner_ref.shape[1:])
    upper = is_upper()

    def pair(p, carry):
        inner, outer = inner_ref[p].astype(jnp.float32), outer_ref[p].astype(jnp.float32)
        lo, hi = jnp.where(upper, inner, outer), jnp.where(upper, outer, inner)
        wide_ref[p, 0] = jnp.where(first, hi, swap_halves(lo))
        wide_ref[p, 1] = jnp.where(first, swap_halves(hi), lo)
        return carry

    lax.fori_loop(0, inner_ref.shape[0], pair, 0, unroll=9)


def in_vmem(x):
    return pltpu.with_memory_space_constraint(x, pltpu.VMEM)


def in_hbm(x):
    return pltpu.with_memory_space_constraint(x, pltpu.HBM)


VMEM = pl.BlockSpec(memory_space=pltpu.VMEM)
ANY = pl.BlockSpec(memory_space=pl.ANY)
SMEM = pl.BlockSpec(memory_space=pltpu.SMEM)
LIMIT = pltpu.CompilerParams(vmem_limit_bytes=2 * 2**20)


def cost(flops, size):
    return pl.CostEstimate(flops=flops, bytes_accessed=size, transcendentals=0)


def packed(coefficients, start):
    pairs = coefficients.reshape(-1, 2, *coefficients.shape[-2:])
    half = pltpu.VMEM((pairs.shape[0], *pairs.shape[2:]), pairs.dtype)
    edge = pltpu.VMEM((start.shape[0], *start.shape[2:]), start.dtype)
    return pl.pallas_call(
        pack,
        out_shape=(
            pltpu.VMEM(pairs.shape, jnp.float32),
            half,
            half,
            pltpu.VMEM(start.shape, start.dtype),
            edge,
            edge,
        ),
        in_specs=[pl.BlockSpec(memory_space=pltpu.HBM)] * 2,
        out_specs=(VMEM,) * 6,
        scratch_shapes=[pltpu.VMEM(pairs.shape, pairs.dtype), pltpu.SemaphoreType.DMA((7,))],
        compiler_params=LIMIT,
        cost_estimate=cost(10**6, 4 * 10**6),
    )(in_hbm(pairs), in_hbm(start))


def unpacked(inner, outer):
    return pl.pallas_call(
        unpack,
        out_shape=pltpu.VMEM((inner.shape[0], 2, *inner.shape[1:]), jnp.float32),
        in_specs=[VMEM] * 2,
        out_specs=VMEM,
        compiler_params=LIMIT,
        cost_estimate=cost(10**6, 4 * 10**6),
    )(in_vmem(inner), in_vmem(outer))


def both_kernel(s_ref, one_ref, two_ref, after_ref, inner_ref, outer_ref):
    odd, upper = is_odd(), is_upper()
    columns = s_ref.shape[1]
    low = half_mask(s_ref.shape[2:])
    for e in range(s_ref.shape[0]):
        one, two = one_ref[e], two_ref[e]
        left, right = jnp.where(odd, one, two), jnp.where(odd, two, one)
        inner_ref[e, :columns] = s_ref[e]
        outer_ref[e, :columns] = s_ref[e]
        up = jnp.where(low, swap_halves(left), right)
        down = jnp.where(low, left, swap_halves(right))
        inner_ref[e, columns] = jnp.where(upper, down, up)
        outer_ref[e, columns] = jnp.where(upper, up, down)


def begin_kernel(
    s_ref, inner_ref, outer_ref, one_ref, two_ref, after_ref, v_ref, first_ref, second_ref
):
    odd, upper = is_odd(), is_upper()
    columns = s_ref.shape[1]
    low = half_mask(s_ref.shape[2:])
    for e in range(s_ref.shape[0]):
        for x in range(columns):
            v_ref[0, e, x] = s_ref[e, x]
            v_ref[1, e, x] = jnp.where(
                upper,
                jnp.where(low, outer_ref[e, x], inner_ref[e, x]),
                jnp.where(low, inner_ref[e, x], outer_ref[e, x]),
            )
        inner, outer = inner_ref[e, columns], outer_ref[e, columns]
        lo, hi = jnp.where(upper, inner, outer), jnp.where(upper, outer, inner)
        left = jnp.where(low, hi, swap_halves(lo))
        right = jnp.where(low, swap_halves(hi), lo)
        first_ref[0, e], second_ref[0, e] = one_ref[e], two_ref[e]
        first_ref[1, e] = jnp.where(odd, left, right)
        second_ref[1, e] = jnp.where(odd, right, left)


def small_call(kernel, outs, *operands, after=()):
    return pl.pallas_call(
        kernel,
        out_shape=tuple(pltpu.VMEM(shape, jnp.float32) for shape in outs),
        in_specs=[VMEM] * len(operands) + [ANY] * len(after),
        out_specs=(VMEM,) * len(outs),
        compiler_params=LIMIT,
        cost_estimate=cost(10**5, 10**5),
    )(*(in_vmem(x) for x in operands), *after)


def early_kernel(e_ref, after_ref, held_ref, sem):
    copy = pltpu.make_async_copy(e_ref, held_ref, sem.at[0])
    copy.start()
    copy.wait()


def held(earlier, after):
    return pl.pallas_call(
        early_kernel,
        out_shape=pltpu.VMEM(earlier.shape, earlier.dtype),
        in_specs=[pl.BlockSpec(memory_space=pltpu.HBM), ANY],
        out_specs=VMEM,
        scratch_shapes=[pltpu.SemaphoreType.DMA((1,))],
        compiler_params=LIMIT,
        cost_estimate=cost(10**5, 5 * 10**6),
    )(in_hbm(earlier), after)


def step_kernel(step, first_step, last_step, shifts_ref, *refs):
    split = len(refs) - (1 if last_step else 3)
    (own_ref, wide_ref, v_ref, one_ref, two_ref, *more), outs = refs[:split], refs[split:]
    odd, upper = is_odd(), is_upper()
    comps, columns = v_ref.shape[1:3]
    rows, lanes = v_ref.shape[3:]
    keep = 1.0 - shifts_ref[step]
    row = lax.broadcasted_iota(jnp.int32, (rows, lanes), 0)
    lane = lax.broadcasted_iota(jnp.int32, (rows, lanes), 1)
    for x in range(columns):
        acc = [[None] * comps for _ in range(1 if last_step else 2)]
        for e in range(comps):
            own, ext = v_ref[0, e, x], v_ref[1, e, x]
            down, up = pltpu.roll(own, 1, 0), pltpu.roll(own, rows - 1, 0)
            ext_down, ext_up = pltpu.roll(ext, 1, 0), pltpu.roll(ext, rows - 1, 0)
            if first_step:
                inner, outer = more[0][e, x], more[1][e, x]
                lo, hi = jnp.where(upper, inner, outer), jnp.where(upper, outer, inner)
                low = row < rows // 2
                wide_down = jnp.where(low, pltpu.roll(hi, 1, 0), pltpu.roll(lo, 1, 0))
                wide_up = jnp.where(low, pltpu.roll(hi, rows - 1, 0), pltpu.roll(lo, rows - 1, 0))
            else:
                wide_down, wide_up = ext_down, ext_up
            below = [jnp.where(row == 0, ext_down, down), jnp.where(row == 0, down, wide_down)]
            above = [
                jnp.where(row == rows - 1, ext_up, up),
                jnp.where(row == rows - 1, up, wide_up),
            ]
            for t, source in enumerate((own_ref, wide_ref)[: len(acc)]):
                center = v_ref[t, e, x]
                fields = [
                    center,
                    below[t],
                    above[t],
                    jnp.where(odd, one_ref[t, e], two_ref[t, e]) if x == 0 else v_ref[t, e, x - 1],
                    jnp.where(odd, two_ref[t, e], one_ref[t, e])
                    if x == columns - 1
                    else v_ref[t, e, x + 1],
                    jnp.where(lane == 0, 0.0, pltpu.roll(center, 1, 1)),
                    jnp.where(lane == lanes - 1, 0.0, pltpu.roll(center, lanes - 1, 1)),
                ]
                for c in range(comps):
                    total = acc[t][c]
                    for d, f in enumerate(fields):
                        term = source[d, c, e, x] * f
                        total = term if total is None else total + term
                    acc[t][c] = total
        for t in range(len(acc)):
            for c in range(comps):
                value = acc[t][c] + keep * v_ref[t, c, x]
                if last_step:
                    outs[0][c, x] = value
                else:
                    outs[0][t, c, x] = value
    if not last_step:
        for t in range(2):
            for c in range(comps):
                near, far = outs[0][t, c, 0], outs[0][t, c, columns - 1]
                outs[1][t, c] = jnp.where(odd, near, far)
                outs[2][t, c] = jnp.where(odd, far, near)


def stepped(step, depth, shifts, own, wide, v, one, two, more, after):
    last = step == depth - 1
    full = pltpu.VMEM(v.shape[1:] if last else v.shape, v.dtype)
    edge = pltpu.VMEM(one.shape, one.dtype)
    return pl.pallas_call(
        lambda *refs: step_kernel(
            step, step == 0, last, *refs[: 6 + len(more)], *refs[6 + len(more) + len(after) :]
        ),
        out_shape=(full,) if last else (full, edge, edge),
        in_specs=[SMEM] + [VMEM] * (5 + len(more)) + [ANY] * len(after),
        out_specs=(VMEM,) if last else (VMEM,) * 3,
        compiler_params=LIMIT,
        cost_estimate=cost(10**7, 3 * 10**6),
    )(shifts, *(in_vmem(a) for a in (own, wide, v, one, two, *more)), *after)


LANES = 128
SLOT = 32
STRIDE = 40


def dots_row(e_ref, w_refs, part):
    count, comps, columns = e_ref.shape[:3]
    v_ref = w_refs[-1]
    part[...] = jnp.zeros_like(part)
    group = 6
    terms = [(e_ref, j) for j in range(count)] + [(w, None) for w in w_refs]
    for at in range(0, len(terms), group):
        some = terms[at : at + group]
        acc = [None] * len(some)
        for c in range(comps):
            for x in range(columns):
                v = v_ref[c, x]
                for n, (ref, j) in enumerate(some):
                    term = v * (ref[c, x] if j is None else ref[j, c, x])
                    acc[n] = term if acc[n] is None else acc[n] + term
        for n, total in enumerate(acc):
            part[at + n : at + n + 1] = jnp.sum(total, axis=0, keepdims=True)
    ones = jnp.ones((8, part.shape[1]), jnp.float32)
    return lax.dot_general(
        ones, part[...], (((1,), (1,)), ((), ())), precision=EXACT,
        preferred_element_type=jnp.float32,
    )[:1]


def dots_kernel(e_ref, *refs):
    *w_refs, out_ref, part = refs
    out_ref[...] = dots_row(e_ref, w_refs, part)


def dots(earlier, vectors):
    return pl.pallas_call(
        dots_kernel,
        out_shape=pltpu.VMEM((1, LANES), jnp.float32),
        in_specs=[VMEM] * (1 + len(vectors)),
        out_specs=VMEM,
        scratch_shapes=[pltpu.VMEM((LANES, LANES), jnp.float32)],
        compiler_params=LIMIT,
        cost_estimate=cost(10**6, 3 * 10**6),
    )(in_vmem(earlier), *(in_vmem(v) for v in vectors))


def lane_roll(x, shift):
    shift %= LANES
    return pltpu.roll(x, shift, 1) if shift else x


def folds(count):
    for j in range(count // 2):
        yield j, count - 1 - j, j // (LANES // SLOT), SLOT * (j % (LANES // SLOT))


def tiles_of(count, block):
    early = -(-(count // 2) * SLOT // LANES)
    per = LANES // STRIDE
    return early, per, early + -(-block // per)


def message_kernel(block, sums, e_ref, *refs):
    w_refs, refs = refs[:block], refs[block:]
    rows, refs = refs[: block - 1], refs[block - 1 :]
    parts, (out_ref, part, square) = refs[:sums], refs[sums:]
    count = e_ref.shape[0]
    early, per, total = tiles_of(count, block)
    square[...] = jnp.zeros_like(square)
    square[:count, :count] = sum(p[...] for p in parts)
    lane = lax.broadcasted_iota(jnp.int32, (1, LANES), 1)
    tiles = [jnp.zeros((1, LANES), jnp.float32) for _ in range(total)]
    for j, r, q, at in folds(count):
        upper = lane_roll(square[j : j + 1], at + 1)
        lower = lane_roll(square[r : r + 1], at - r)
        tiles[q] = jnp.where(
            (lane > at + j) & (lane <= at + count),
            upper,
            jnp.where((lane >= at) & (lane <= at + j), lower, tiles[q]),
        )
    last = dots_row(e_ref, w_refs, part)
    for k in range(block):
        row = last if k == block - 1 else rows[k][...]
        t = early + k // per
        tiles[t] = tiles[t] + lane_roll(row, STRIDE * (k % per))
    for t in range(total):
        out_ref[:, t * LANES : (t + 1) * LANES] = tiles[t]


def message(earlier, vectors, rows, parts):
    count, block = earlier.shape[0], len(vectors)
    width = LANES * tiles_of(count, block)[2]
    operands = (earlier, *vectors, *rows, *parts)
    return pl.pallas_call(
        lambda *refs: message_kernel(block, len(parts), *refs),
        out_shape=pltpu.VMEM((1, width), jnp.float32),
        in_specs=[VMEM] * len(operands),
        out_specs=VMEM,
        scratch_shapes=[
            pltpu.VMEM((LANES, LANES), jnp.float32),
            pltpu.VMEM((SLOT, LANES), jnp.float32),
        ],
        compiler_params=LIMIT,
        cost_estimate=cost(10**6, 3 * 10**6),
    )(*(in_vmem(x) for x in operands))


def against(a, b):
    return lax.dot_general(
        a, b, (((1,), (1,)), ((), ())), precision=EXACT, preferred_element_type=jnp.float32
    )


def finish(block, scale, m_ref, e_ref, *refs):
    w_refs, refs = refs[:block], refs[block:]
    out_ref, proj_ref, tri_ref, o_vmem, small, turned_vmem, square, lines, spread, sems = refs
    count = e_ref.shape[0]
    early, per, total = tiles_of(count, block)
    tiles = [
        jnp.sum(m_ref[:, t * LANES : (t + 1) * LANES], axis=0, keepdims=True) * scale
        for t in range(total)
    ]
    lane = lax.broadcasted_iota(jnp.int32, (1, LANES), 1)
    for k in range(block):
        lines[k : k + 1] = lane_roll(tiles[early + k // per], -STRIDE * (k % per))
    for j, r, q, at in folds(count):
        upper = jnp.where(lane >= j, lane_roll(tiles[q], -at - 1), 0.0)
        lower = jnp.where(lane >= r, lane_roll(tiles[q], r - at), 0.0)
        square[j : j + 1] = jnp.where(lane == j, 0.5 * upper, upper)
        square[r : r + 1] = jnp.where(lane == r, 0.5 * lower, lower)
    turned = lines[:block, :count]
    turned_vmem[...] = turned
    proj = pltpu.make_async_copy(turned_vmem, proj_ref, sems.at[0])
    proj.start()
    row = lax.broadcasted_iota(jnp.int32, (block, block), 0)
    col = lax.broadcasted_iota(jnp.int32, (block, block), 1)
    unit = jnp.where(row == col, 1.0, 0.0)
    inner = lines[:block, count : count + block]
    inner = jnp.where(row > col, inner, jnp.where(row == col, 0.5 * inner, 0.0))
    part = jnp.dot(turned, square[:count, :count], precision=EXACT) - turned
    gram = inner + against(part, turned)
    gram = gram + against(unit, gram)
    a = jnp.concatenate([gram, unit, -turned], axis=1)
    rows = lax.broadcasted_iota(jnp.int32, a.shape, 0)
    for k in range(block):
        inverse = 1.0 / jnp.sqrt(a[k : k + 1, k : k + 1])
        pivot = a[k : k + 1] * inverse
        factor = a[:, k : k + 1] * inverse
        a = jnp.where(rows == k, pivot, jnp.where(rows > k, a - factor * pivot, a))
    small[...] = jnp.where(row <= col, a[:, :block], 0.0)
    tri = pltpu.make_async_copy(small, tri_ref, sems.at[1])
    tri.start()
    shape = spread.shape[2:]
    for k in range(block):
        for i in range(block + count):
            if i >= block or i <= k:
                at = block + i
                spread[i, k] = jnp.broadcast_to(a[k : k + 1, at : at + 1], shape)
    outs = []
    comps = 2
    for g in range(e_ref.shape[1] // comps):
        sel = slice(g * comps, (g + 1) * comps)
        acc = [None] * block
        for i in range(block + count):
            x = w_refs[i][sel] if i < block else e_ref[i - block, sel]
            for k in range(block):
                if i >= block or i <= k:
                    t = spread[i, k][None, None] * x
                    acc[k] = t if acc[k] is None else acc[k] + t
        for k in range(block):
            o_vmem[g, k] = acc[k]
        c = pltpu.make_async_copy(o_vmem.at[g], out_ref.at[:, sel], sems.at[2 + g])
        c.start()
        outs.append(c)
    for c in [proj, tri, *outs]:
        c.wait()


def finished(everything, total, vectors, earlier):
    block, count = len(vectors), earlier.shape[0]
    fields, *rest = vectors[0].shape
    operands = (everything, earlier, *vectors)
    return pl.pallas_call(
        lambda *refs: finish(block, 1.0 / total, *refs),
        out_shape=(
            pltpu.HBM((block, fields, *rest), jnp.float32),
            pltpu.HBM((block, count), jnp.float32),
            pltpu.HBM((block, block), jnp.float32),
        ),
        in_specs=[VMEM] * len(operands),
        out_specs=(pl.BlockSpec(memory_space=pltpu.HBM),) * 3,
        scratch_shapes=[
            pltpu.VMEM((fields // 2, block, 2, *rest), jnp.float32),
            pltpu.VMEM((block, block), jnp.float32),
            pltpu.VMEM((block, count), jnp.float32),
            pltpu.VMEM((SLOT, LANES), jnp.float32),
            pltpu.VMEM((8, LANES), jnp.float32),
            pltpu.VMEM((block + count, block, *rest[1:]), jnp.float32),
            pltpu.SemaphoreType.DMA((2 + fields // 2,)),
        ],
        compiler_params=LIMIT,
        cost_estimate=cost(10**7, 3 * 10**6),
    )(*(in_vmem(x) for x in operands))


def body(coefficients, earlier, start, shifts):
    depth = shifts.shape[0]
    coefficients = jnp.transpose(coefficients, (0, 1, 2, 4, 3, 5))
    earlier = jnp.transpose(earlier, (0, 1, 3, 2, 4))
    start = jnp.transpose(start, (0, 2, 1, 3))
    slabs = lax.axis_size(SLAB)
    inside = [(i, i ^ 1) for i in range(slabs)]
    outside = [(i, ((i + 1) ^ 1) - 1) for i in range(1, slabs - 1)]
    columns = lax.axis_size("sub")
    pairs = [(i, i ^ 1) for i in range(columns)]
    between = [(i, ((i + 1) ^ 1) - 1) for i in range(1, columns - 1)]
    own, inner, outer, start, one, two = packed(coefficients, start)
    inner = lax.ppermute(inner, SLAB, inside)
    outer = lax.ppermute(outer, SLAB, outside)
    fields, width, *plane = start.shape
    from_one = lax.ppermute(one, "sub", pairs)
    from_two = lax.ppermute(two, "sub", between)
    earlier = held(earlier, one)
    s_inner, s_outer = small_call(
        both_kernel, [(fields, width + 1, *plane)] * 2, start, from_one, from_two, after=(earlier,)
    )
    s_inner = lax.ppermute(s_inner, SLAB, inside)
    s_outer = lax.ppermute(s_outer, SLAB, outside)
    own = own.reshape(coefficients.shape)
    wide = unpacked(inner, outer).reshape(coefficients.shape)
    v, from_one, from_two = small_call(
        begin_kernel,
        [(2, *start.shape)] + [(2, fields, *plane)] * 2,
        start, s_inner, s_outer, from_one, from_two, after=(wide,),
    )
    vectors, rows, early = [start], [], []
    thirds = earlier.shape[1] // 3
    for step in range(depth):
        if step:
            from_one = lax.ppermute(one, "sub", pairs)
            from_two = lax.ppermute(two, "sub", between)
        more = (s_inner, s_outer) if step == 0 else ()
        after = []
        if step:
            rows.append(dots(earlier, vectors))
            after.append(rows[-1])
        if step == depth - 1:
            rows.insert(0, dots(earlier, vectors[:1]))
            after.append(rows[0])
        if 1 <= step <= 3:
            tied, v = lax.optimization_barrier((earlier, v))
            some = tied[:, (step - 1) * thirds : step * thirds].reshape(tied.shape[0], -1)
            early.append(lax.optimization_barrier(jnp.dot(some, some.T, precision=EXACT)))
            after.append(early[-1])
        out = stepped(step, depth, shifts, own, wide, v, from_one, from_two, more, after)
        if step < depth - 1:
            v, one, two = out
            vectors.append(v[0])
        else:
            vectors.append(out[0])
    total = start.size * lax.axis_size(SLAB) * lax.axis_size("sub")
    near = over_copies(message(earlier, vectors, rows, early), NEAR)
    everything = all_copies(near, FAR)[:, 0]
    new, projection, triangle = finished(everything, total, vectors, earlier)
    return (jnp.transpose(new, (0, 1, 3, 2, 4)), projection.T, triangle)


def solution(mesh):
    torus = Mesh(
        mesh.devices.reshape(4, 16, 2, mesh.shape["sub"]), ("slab_0", "slab_1", "slab_2", "sub")
    )
    return jax.shard_map(
        body,
        mesh=torus,
        in_specs=(
            P(None, None, None, SLAB, "sub", None),
            P(None, None, SLAB, "sub", None),
            P(None, SLAB, "sub", None),
            P(),
        ),
        out_specs=(P(None, None, SLAB, "sub", None), P(), P()),
        check_vma=False,
    )
```
